32 devices in a mesh: dp: 2 (over y), mp: 16 (over z, x, core).
Axes of the slice: x: 2, y: 2, z: 4, core: 2. Of those that a mesh axis runs over, the one named last changes fastest.
Arguments:
- attn_out: bfloat16 [1024, 8192], P('dp', 'mp'), may hold values from -6 to 6
- grad_out: bfloat16 [1024, 8192], P(('dp', 'mp')), may hold values from -0.26367188 to 0.26367188
- proj_weight: bfloat16 [8192, 8192], P('mp'), may hold values from -1.5 to 1.5
- error_buf: bfloat16 [2, 8192, 8192], P('dp', 'mp'), may hold values from -6 to 6
- q_start: float32 [8192, 32], P('mp'), may hold values from -6 to 6
Outputs:
- new_error: bfloat16 [2, 8192, 8192], P('dp', 'mp')
- q_factor: float32 [8192, 32], P('mp')
- d_attn: bfloat16 [1024, 8192], P('dp', 'mp')
The draws below stay inside these ranges and needn't reach their ends.
All inputs are finite; a program needn't handle non-finite values.
Results may differ from the reference program's by a relative error of at most 0.012.
Values may be sent and summed in bfloat16 or wider, within the bound.
A program may use at most 128 MiB of HBM per device.

```python
import jax
import jax.numpy as jnp
from jax import lax

D = 8192
R = 32
TOK_REP = 512
TOKENS = 1024
N_DP = 2


def steps_of(key, extent, shards, low, high):
    level = 1.0
    for position, parts in shards:
        heights = jax.random.uniform(jax.random.fold_in(jax.random.fold_in(key, 6), position), (parts,), jnp.float32, low / len(shards), high / len(shards))
        level = level * jnp.repeat(jnp.exp(heights), extent[position] // parts).reshape((-1,) + (1,) * (len(extent) - 1 - position))
    return level


def scatter_about(stream_key, shape, width, limit, pieces=(), dtype=jnp.bfloat16):
    entries = width * jax.random.normal(stream_key, shape, jnp.float32)
    if pieces:
        entries = entries * steps_of(stream_key, shape, pieces, -0.22, 0.18)
    return jnp.clip(entries, -limit, limit).astype(dtype)


def setup_inputs(seed: int = 0) -> dict:
    key_list = jax.random.split(jax.random.key(seed), 6)
    attn_out = scatter_about(key_list[0], (TOKENS, D), 1.0, 6.0, ((0, 2), (1, 16)))
    grad_out = scatter_about(key_list[1], (TOKENS, D), (TOK_REP ** -0.5), 0.26367188, ((0, 32),))
    proj_weight = scatter_about(key_list[2], (D, D), (TOK_REP ** 0.5 * D ** -0.5), 1.5, ((0, 16),))
    error_buf = scatter_about(key_list[3], (N_DP, D, D), 1.0, 6.0, ((0, 2), (1, 16)))
    q_start = scatter_about(key_list[4], (D, R), 1.0, 6.0, ((0, 16),), jnp.float32)
    return {"attn_out": attn_out, "grad_out": grad_out, "proj_weight": proj_weight, "error_buf": error_buf, "q_start": q_start}


def reference(attn_out, grad_out, proj_weight, error_buf, q_start):
    hp = lax.Precision.HIGHEST
    d_attn = lax.dot_general(grad_out.astype(jnp.float32), proj_weight.astype(jnp.float32), (((1,), (1,)), ((), ())), preferred_element_type=jnp.float32).astype(jnp.bfloat16)
    moments = []
    p_total = jnp.zeros((D, R), jnp.float32)
    for replica in range(N_DP):
        rows_a = attn_out[replica * TOK_REP:(replica + 1) * TOK_REP]
        rows_g = grad_out[replica * TOK_REP:(replica + 1) * TOK_REP]
        gradient = jnp.dot(rows_a.T.astype(jnp.float32), rows_g.astype(jnp.float32), preferred_element_type=jnp.float32)
        moment = gradient + error_buf[replica].astype(jnp.float32)
        moments.append(moment)
        p_total = p_total + jnp.dot(moment, q_start, precision=hp)
    p_mean = p_total / N_DP
    gram_sum = jnp.dot(p_mean.T, p_mean, precision=hp)
    lower_factor = jnp.linalg.cholesky(gram_sum)
    p_ortho = lax.linalg.triangular_solve(lower_factor, p_mean, left_side=False, lower=True, transpose_a=True)
    q_total = jnp.zeros((D, R), jnp.float32)
    for replica in range(N_DP):
        q_total = q_total + jnp.dot(moments[replica].T, p_ortho, precision=hp)
    q_factor = q_total / N_DP
    approx = jnp.dot(p_ortho, q_factor.T, precision=hp)
    errors = []
    for replica in range(N_DP):
        errors.append((moments[replica] - approx).astype(jnp.bfloat16))
    return (jnp.stack(errors), q_factor, d_attn)
```

```python
import functools

import jax
import jax.numpy as jnp
from jax import lax
from jax.experimental import pallas as pl
from jax.experimental.pallas import tpu as pltpu
from jax.sharding import PartitionSpec as P

MESH = pl.DeviceIdType.MESH
HP = lax.Precision.HIGHEST
F32, BF16 = jnp.float32, jnp.bfloat16
NN = (((1,), (0,)), ((), ()))
NT = (((1,), (1,)), ((), ()))
TN = (((0,), (0,)), ((), ()))
NC, NZ = 2, 4


def dot(a, b, dims, precision=None):
    return lax.dot_general(a, b, dims, precision=precision, preferred_element_type=F32)


def split(v):
    hi = v.astype(BF16)
    return hi, (v - hi.astype(F32)).astype(BF16)


def inverse_of_factor(gram):
    r = gram.shape[0]
    rows = lax.broadcasted_iota(jnp.int32, (r, 1), 0)
    eye = (rows == lax.broadcasted_iota(jnp.int32, (r, r), 1)).astype(F32)
    low, pivots = eye, jnp.ones((r, 1), F32)
    for k in range(r):
        pivot = gram[k:k + 1, k:k + 1]
        pivots = jnp.where(rows == k, pivot, pivots)
        factor = jnp.where(rows > k, gram[:, k:k + 1] / pivot, 0.0)
        low = low - factor * low[k:k + 1, :]
        gram = gram - factor * gram[k:k + 1, :]
    return low * lax.rsqrt(pivots)


def chain_kernel(n_dp, n_mp, t,
                 a_ref, g_hbm, e_hbm, q_ref,
                 gout, pp_ref, qq_ref, qown_ref,
                 e_ref, g_ref, qb, gqb, pb, sacc, gacc, qacc, qdp, q2b,
                 s1, r1, s2, r2, s3, r3, m1, m2, m3, t1, t2, t3, u1, u2, u3, gr,
                 send, recv, gsend, grecv, local):
    nx = n_mp // (NC * NZ)
    half = nx * NZ
    d, m = lax.axis_index("dp"), lax.axis_index("mp")
    c = lax.rem(m, NC)
    x = lax.rem(lax.div(m, NC), nx)
    z = lax.div(m, NC * nx)
    f = a_ref.shape[1]
    rank = q_ref.shape[1]

    def dev(zz=None, xx=None, cc=None):
        zz, xx, cc = (z if zz is None else zz), (x if xx is None else xx), (c if cc is None else cc)
        return (d, (zz * nx + xx) * NC + cc)

    def slot(zz, xx, cc):
        return (cc * nx + xx) * NZ + zz

    slots = [slot(i // (NC * nx), (i // NC) % nx, i % NC) for i in range(n_mp)]
    z_peers = [lax.rem(z + k, NZ) for k in range(1, NZ)]
    x_peers = [lax.rem(x + k, nx) for k in range(1, nx)]
    d_peers = [lax.rem(d + k, n_dp) for k in range(1, n_dp)]
    own = slot(z, x, c)

    e_copy = pltpu.make_async_copy(e_hbm.at[0], e_ref, local.at[0])
    g_copy = pltpu.make_async_copy(g_hbm, g_ref, local.at[1])
    own_rows = pl.ds(pl.multiple_of(m * t, t), t)
    o_copy = pltpu.make_async_copy(g_hbm, gout.at[own_rows, :], local.at[2])
    g_copy.start()
    e_copy.start()
    o_copy.start()

    barrier = pltpu.get_barrier_semaphore()
    for peer in ([dev(zz=p) for p in z_peers] + [dev(xx=p) for p in x_peers]
                 + [dev(cc=1 - c)] + [(p, m) for p in d_peers]):
        pl.semaphore_signal(barrier, inc=1, device_id=peer, device_id_type=MESH)
    pl.semaphore_wait(barrier, NZ + nx - 1 + n_dp - 1)

    used = [0]

    def push(src, dst, peer):
        i = used[0]
        used[0] += 1
        copy = pltpu.make_async_remote_copy(
            src_ref=src, dst_ref=dst, send_sem=send.at[i], recv_sem=recv.at[i],
            device_id=peer, device_id_type=MESH)
        copy.start()
        return copy

    def wait(copies):
        for copy in copies:
            copy.wait()

    def rows_of(zz, xx, cc):
        return pl.ds(pl.multiple_of(((zz * nx + xx) * NC + cc) * t, t), t)

    def bulk(zz, xx, cc, kind, peer, src=None):
        at = gout.at[rows_of(zz, xx, cc), :]
        i = slot(zz, xx, cc)
        return pltpu.make_async_remote_copy(
            src_ref=at if src is None else src, dst_ref=at,
            send_sem=gsend.at[kind, i], recv_sem=grecv.at[i],
            device_id=peer, device_id_type=MESH)

    k_core = 1 + nx

    def spread(zz, src=None):
        for k, p in enumerate(x_peers):
            bulk(zz, x, c, 2 + k, dev(xx=p), src).start()
        bulk(zz, x, c, k_core, dev(cc=1 - c), src).start()

    def up(zz, src=None):
        @pl.when(z < NZ - 1)
        def _():
            bulk(zz, x, c, 0, dev(zz=lax.min(z + 1, NZ - 1)), src).start()

    def down(zz, src=None):
        @pl.when(z > 0)
        def _():
            bulk(zz, x, c, 1, dev(zz=lax.max(z - 1, 0)), src).start()

    def arrived(zz, xx, cc):
        bulk(zz, xx, cc, 0, dev(cc=1 - c)).wait_recv()

    def hop(s):
        @pl.when(z >= s)
        def _():
            zz = z - s
            arrived(zz, x, c)
            up(zz)
            spread(zz)

        @pl.when(z + s < NZ)
        def _():
            zz = z + s
            arrived(zz, x, c)
            down(zz)
            spread(zz)

    def across(s):
        for p in x_peers:
            for zz, ok in ((z - s, z >= s), (z + s, z + s < NZ)):
                if s == 0:
                    ok = zz >= 0

                @pl.when(ok)
                def _(zz=zz, p=p):
                    arrived(zz, p, c)
                    bulk(zz, p, c, k_core, dev(cc=1 - c)).start()
                if s == 0:
                    break

    qb[own] = jnp.transpose(q_ref[...]).astype(BF16)
    copies = [push(qb.at[own], qb.at[own], dev(zz=p)) for p in z_peers]
    up(z, g_hbm)
    down(z, g_hbm)
    spread(z, g_hbm)
    wait(copies)
    line = pl.ds(slot(0, x, c), NZ)
    wait([push(qb.at[line], qb.at[line], dev(xx=p)) for p in x_peers])
    plane = pl.ds(slot(0, 0, c), half)
    wait([push(qb.at[plane], qb.at[plane], dev(cc=1 - c))])

    g_copy.wait()
    gq = jnp.zeros((t, rank), F32)
    for i, s in enumerate(slots):
        gq += dot(g_ref[:, i * f:(i + 1) * f], qb[s], NT)
    gqb[own] = gq
    copies = [push(gqb.at[own], gqb.at[own], dev(zz=p)) for p in z_peers]
    e_copy.wait()
    pt = jnp.zeros((rank, f), F32)
    for i, s in enumerate(slots):
        pt += dot(qb[s], e_ref[:, i * f:(i + 1) * f], NT)
    wait(copies)
    wait([push(gqb.at[line], gqb.at[line], dev(xx=p)) for p in x_peers])
    wait([push(gqb.at[plane], gqb.at[plane], dev(cc=1 - c))])
    gq_all = jnp.concatenate([gqb[s] for s in slots], axis=0)
    hi, lo = split(gq_all)
    a = a_ref[...]
    pt += dot(hi, a, TN) + dot(lo, a, TN)
    pb[d] = pt
    wait([push(pb.at[d], pb.at[d], (p, m)) for p in d_peers])
    pt = pb[0]
    for k in range(1, n_dp):
        pt += pb[k]
    pt = pt / n_dp

    p_hi, p_lo = split(pt)
    sums = dot(a, p_hi, NT) + dot(a, p_lo, NT)
    for i, s in enumerate(slots):
        sacc[s] = sums[i * t:(i + 1) * t]
    gacc[...] = dot(pt, pt, NT, HP)

    def reduce(acc, bs, br, dtype, extra):
        s_c, s_x, s_z = bs
        r_c, r_x, r_z = br
        s_c[...] = acc[pl.ds(slot(0, 0, 1 - c), half)].astype(dtype)
        copies = [push(s_c, r_c, dev(cc=1 - c))]
        if extra:
            m1[...] = gacc[...]
            copies.append(push(m1, gr.at[0], dev(cc=1 - c)))
        wait(copies)
        mine = pl.ds(slot(0, 0, c), half)
        acc[mine] = acc[mine] + r_c[...].astype(F32)
        copies = []
        if extra:
            m2[...] = gacc[...] + gr[0]
        for k, p in enumerate(x_peers):
            s_x[k] = acc[pl.ds(slot(0, p, c), NZ)].astype(dtype)
            copies.append(push(s_x.at[k], r_x.at[k], dev(xx=p)))
            if extra:
                copies.append(push(m2, gr.at[1 + k], dev(xx=p)))
        wait(copies)
        mine = pl.ds(slot(0, x, c), NZ)
        for k in range(nx - 1):
            acc[mine] = acc[mine] + r_x[k].astype(F32)
        copies = []
        if extra:
            total = m2[...]
            for k in range(nx - 1):
                total = total + gr[1 + k]
            m3[...] = total
        for k, p in enumerate(z_peers):
            s_z[k] = acc[slot(p, x, c)].astype(dtype)
            copies.append(push(s_z.at[k], r_z.at[k], dev(zz=p)))
            if extra:
                copies.append(push(m3, gr.at[nx + k], dev(zz=p)))
        wait(copies)
        out = acc[own]
        for k in range(NZ - 1):
            out = out + r_z[k].astype(F32)
        if not extra:
            return out
        total = m3[...]
        for k in range(NZ - 1):
            total = total + gr[nx + k]
        return out, total

    s_own, gram = reduce(sacc, (t1, t2, t3), (r1, r2, r3), F32, True)
    hop(1)
    across(0)

    inv = inverse_of_factor(gram)
    pot = dot(inv, pt, NN, HP)
    o_hi, o_lo = split(-pot)
    pp_ref[:rank, :] = o_hi
    pp_ref[rank:, :] = o_lo
    so_hi, so_lo = split(dot(inv, s_own, NT, HP))
    stack = jnp.concatenate([o_hi, o_lo], axis=0)
    s_stack = jnp.concatenate([so_hi, so_lo], axis=0)
    for i, s in enumerate(slots):
        cols = slice(i * f, (i + 1) * f)
        part = dot(s_stack, g_ref[:, cols], NN) - dot(stack, e_ref[:, cols], NN)
        qacc[s] = part[:rank] + part[rank:]
    hop(2)
    across(1)
    q_sum = reduce(qacc, (s1, s2, s3), (u1, u2, u3), BF16, False)
    qdp[d] = q_sum
    wait([push(qdp.at[d], qdp.at[d], (p, m)) for p in d_peers])
    q_own = qdp[0]
    for k in range(1, n_dp):
        q_own += qdp[k]
    q_own = q_own / n_dp
    qown_ref[...] = q_own
    hop(3)
    across(2)

    q2b[own] = q_own.astype(BF16)
    wait([push(q2b.at[own], q2b.at[own], dev(zz=p)) for p in z_peers])
    wait([push(q2b.at[line], q2b.at[line], dev(xx=p)) for p in x_peers])
    wait([push(q2b.at[plane], q2b.at[plane], dev(cc=1 - c))])
    for i, s in enumerate(slots):
        qq_ref[:rank, i * f:(i + 1) * f] = q2b[s]
        qq_ref[rank:, i * f:(i + 1) * f] = q2b[s]

    across(3)
    for zz in range(NZ):
        for xx in range(nx):
            arrived(zz, xx, 1 - c)
    for zz in range(NZ):
        @pl.when((zz <= z) & (z < NZ - 1))
        def _(zz=zz):
            bulk(zz, x, c, 0, dev(cc=1 - c)).wait_send()

        @pl.when((zz >= z) & (z > 0))
        def _(zz=zz):
            bulk(zz, x, c, 1, dev(cc=1 - c)).wait_send()
        for k in range(nx - 1):
            bulk(zz, x, c, 2 + k, dev(cc=1 - c)).wait_send()
        for xx in range(nx):
            bulk(zz, xx, c, k_core, dev(cc=1 - c)).wait_send()
    o_copy.wait()


def chain(n_dp, n_mp, attn_out, grad_out, error_buf, q_start):
    t, width = grad_out.shape
    tokens, f = attn_out.shape
    rank = q_start.shape[1]
    nx = n_mp // (NC * NZ)
    half = nx * NZ
    per = NZ - 1 + nx - 1 + 1
    count = 7 * per + 2 * (n_dp - 1)
    any_space = pl.BlockSpec(memory_space=pl.ANY)
    vmem = pl.BlockSpec(memory_space=pltpu.VMEM)
    other = max(nx - 1, 1)
    square = (rank, rank)
    block, tok = (rank, f), (t, rank)
    scratch = [
        pltpu.VMEM((f, width), BF16),
        pltpu.VMEM((t, width), BF16),
        pltpu.VMEM((n_mp,) + block, BF16),
        pltpu.VMEM((n_mp,) + tok, F32),
        pltpu.VMEM((n_dp,) + block, F32),
        pltpu.VMEM((n_mp,) + tok, F32),
        pltpu.VMEM(square, F32),
        pltpu.VMEM((n_mp,) + block, F32),
        pltpu.VMEM((n_dp,) + block, F32),
        pltpu.VMEM((n_mp,) + block, BF16),
        pltpu.VMEM((half,) + block, BF16),
        pltpu.VMEM((half,) + tok, F32),
        pltpu.VMEM((other, NZ) + block, BF16),
        pltpu.VMEM((other, NZ) + tok, F32),
        pltpu.VMEM((NZ - 1,) + block, BF16),
        pltpu.VMEM((NZ - 1,) + tok, F32),
        pltpu.VMEM(square, F32), pltpu.VMEM(square, F32), pltpu.VMEM(square, F32),
        pltpu.VMEM((half,) + tok, F32),
        pltpu.VMEM((other, NZ) + tok, F32),
        pltpu.VMEM((NZ - 1,) + tok, F32),
        pltpu.VMEM((half,) + block, BF16),
        pltpu.VMEM((other, NZ) + block, BF16),
        pltpu.VMEM((NZ - 1,) + block, BF16),
        pltpu.VMEM((nx + NZ - 1,) + square, F32),
        pltpu.SemaphoreType.DMA((count,)),
        pltpu.SemaphoreType.DMA((count,)),
        pltpu.SemaphoreType.DMA((2 + nx, n_mp)),
        pltpu.SemaphoreType.DMA((n_mp,)),
        pltpu.SemaphoreType.DMA((3,)),
    ]
    return pl.pallas_call(
        functools.partial(chain_kernel, n_dp, n_mp, t),
        out_shape=(
            jax.ShapeDtypeStruct((tokens, width), BF16),
            jax.ShapeDtypeStruct((2 * rank, f), BF16),
            jax.ShapeDtypeStruct((2 * rank, width), BF16),
            jax.ShapeDtypeStruct((rank, f), F32),
        ),
        in_specs=[vmem, any_space, any_space, vmem],
        out_specs=(any_space, vmem, vmem, vmem),
        scratch_shapes=scratch,
        compiler_params=pltpu.CompilerParams(
            collective_id=0, has_side_effects=True, vmem_limit_bytes=40 * 2**20),
    )(attn_out, grad_out, error_buf, q_start)


def final_kernel(a_ref, pp_ref, qown_ref, g_ref, w_ref, e_ref, qq_ref,
                 err_ref, q_ref, da_ref, lhs, acc):
    j = pl.program_id(0)
    tokens = a_ref.shape[0]

    @pl.when(j == 0)
    def _():
        lhs[:, :tokens] = jnp.transpose(a_ref[...])
        lhs[:, tokens:] = jnp.transpose(pp_ref[...])
        q_ref[...] = jnp.transpose(qown_ref[...])
        acc[...] = jnp.zeros_like(acc)

    g = g_ref[...]
    moment = dot(lhs[:, :tokens], g, NN) + e_ref[0].astype(F32)
    err_ref[0] = (moment + dot(lhs[:, tokens:], qq_ref[...], NN)).astype(BF16)
    acc[...] += dot(g, w_ref[...], NT)

    @pl.when(j == pl.num_programs(0) - 1)
    def _():
        da_ref[...] = acc[...].astype(BF16)


def final(attn_out, pp, qown, g_all, proj_weight, error_buf, qq):
    tokens, f = attn_out.shape
    width = g_all.shape[1]
    rank = qown.shape[0]
    n = 1024
    whole = lambda shape: pl.BlockSpec(shape, lambda j: (0,) * len(shape))
    cols = lambda rows: pl.BlockSpec((rows, n), lambda j: (0, j))
    cols3 = pl.BlockSpec((1, f, n), lambda j: (0, 0, j))
    return pl.pallas_call(
        final_kernel,
        grid=(width // n,),
        out_shape=(
            jax.ShapeDtypeStruct((1, f, width), BF16),
            jax.ShapeDtypeStruct((f, rank), F32),
            jax.ShapeDtypeStruct((tokens, f), BF16),
        ),
        in_specs=[whole((tokens, f)), whole((2 * rank, f)), whole((rank, f)),
                  cols(tokens), cols(f), cols3, cols(2 * rank)],
        out_specs=(cols3, whole((f, rank)), whole((tokens, f))),
        scratch_shapes=[pltpu.VMEM((f, tokens + 2 * rank), BF16), pltpu.VMEM((tokens, f), F32)],
        compiler_params=pltpu.CompilerParams(vmem_limit_bytes=40 * 2**20),
    )(attn_out, pp, qown, g_all, proj_weight, error_buf, qq)


def on_device(n_dp, n_mp, attn_out, grad_out, proj_weight, error_buf, q_start):
    g_all, pp, qq, qown = chain(n_dp, n_mp, attn_out, grad_out, error_buf, q_start)
    return final(attn_out, pp, qown, g_all, proj_weight, error_buf, qq)


def solution(mesh):
    in_specs = (
        P("dp", "mp"),
        P(("dp", "mp"), None),
        P("mp", None),
        P("dp", "mp", None),
        P("mp", None),
    )
    out_specs = (P("dp", "mp", None), P("mp", None), P("dp", "mp"))
    return jax.shard_map(
        functools.partial(on_device, mesh.shape["dp"], mesh.shape["mp"]),
        mesh=mesh, in_specs=in_specs, out_specs=out_specs, check_vma=False,
    )
```

```python
import functools

import jax
import jax.numpy as jnp
from jax import lax
from jax.experimental import pallas as pl
from jax.experimental.pallas import tpu as pltpu
from jax.sharding import PartitionSpec as P

MESH = pl.DeviceIdType.MESH
HP = lax.Precision.HIGHEST
F32, BF16 = jnp.float32, jnp.bfloat16
NN = (((1,), (0,)), ((), ()))
NT = (((1,), (1,)), ((), ()))
TN = (((0,), (0,)), ((), ()))
NC, NZ = 2, 4


def dot(a, b, dims, precision=None):
    return lax.dot_general(a, b, dims, precision=precision, preferred_element_type=F32)


def split(v):
    hi = v.astype(BF16)
    return hi, (v - hi.astype(F32)).astype(BF16)


def inverse_of_factor(gram):
    r = gram.shape[0]
    rows = lax.broadcasted_iota(jnp.int32, (r, 1), 0)
    eye = (rows == lax.broadcasted_iota(jnp.int32, (r, r), 1)).astype(F32)
    low, pivots = eye, jnp.ones((r, 1), F32)
    for k in range(r):
        pivot = gram[k:k + 1, k:k + 1]
        pivots = jnp.where(rows == k, pivot, pivots)
        factor = jnp.where(rows > k, gram[:, k:k + 1] / pivot, 0.0)
        low = low - factor * low[k:k + 1, :]
        gram = gram - factor * gram[k:k + 1, :]
    return low * lax.rsqrt(pivots)


def chain_kernel(n_dp, n_mp, t,
                 a_ref, g_hbm, e_hbm, q_ref,
                 gout, pp_ref, qq_ref, qown_ref,
                 e_ref, g_ref, qb, gqb, pb, sx, rx, qacc, qdp, q2b, s1, u1, s2, u2,
                 send, recv, gsend, grecv, local):
    nx = n_mp // (NC * NZ)
    half = nx * NZ
    d, m = lax.axis_index("dp"), lax.axis_index("mp")
    c = lax.rem(m, NC)
    x = lax.rem(lax.div(m, NC), nx)
    z = lax.div(m, NC * nx)
    f = a_ref.shape[1]
    rank = q_ref.shape[0]

    def dev(zz=None, xx=None, cc=None):
        zz, xx, cc = (z if zz is None else zz), (x if xx is None else xx), (c if cc is None else cc)
        return (d, (zz * nx + xx) * NC + cc)

    def slot(zz, xx, cc):
        return (cc * nx + xx) * NZ + zz

    slots = [slot(i // (NC * nx), (i // NC) % nx, i % NC) for i in range(n_mp)]
    x_peers = [lax.rem(x + k, nx) for k in range(1, nx)]
    d_peers = [lax.rem(d + k, n_dp) for k in range(1, n_dp)]
    own = slot(z, x, c)

    e_copy = pltpu.make_async_copy(e_hbm.at[0], e_ref, local.at[0])
    g_copy = pltpu.make_async_copy(g_hbm, g_ref, local.at[1])
    own_rows = pl.ds(pl.multiple_of(m * t, t), t)
    o_copy = pltpu.make_async_copy(g_hbm, gout.at[own_rows, :], local.at[2])
    g_copy.start()
    e_copy.start()
    o_copy.start()

    barrier = pltpu.get_barrier_semaphore()
    for k in range(1, n_mp):
        pl.semaphore_signal(barrier, inc=1, device_id=(d, lax.rem(m + k, n_mp)), device_id_type=MESH)
    for p in d_peers:
        pl.semaphore_signal(barrier, inc=1, device_id=(p, m), device_id_type=MESH)
    pl.semaphore_wait(barrier, n_mp - 1 + n_dp - 1)

    used = [0]

    def push(src, dst, peer):
        i = used[0]
        used[0] += 1
        copy = pltpu.make_async_remote_copy(
            src_ref=src, dst_ref=dst, send_sem=send.at[i], recv_sem=recv.at[i],
            device_id=peer, device_id_type=MESH)
        copy.start()
        return copy

    def wait(copies):
        for copy in copies:
            copy.wait()

    def rows_of(zz, xx, cc):
        return pl.ds(pl.multiple_of(((zz * nx + xx) * NC + cc) * t, t), t)

    def bulk(zz, xx, cc, kind, peer, src=None):
        at = gout.at[rows_of(zz, xx, cc), :]
        i = slot(zz, xx, cc)
        return pltpu.make_async_remote_copy(
            src_ref=at if src is None else src, dst_ref=at,
            send_sem=gsend.at[kind, i], recv_sem=grecv.at[i],
            device_id=peer, device_id_type=MESH)

    k_core = 1 + nx

    def spread(zz, src=None):
        for k, p in enumerate(x_peers):
            bulk(zz, x, c, 2 + k, dev(xx=p), src).start()
        bulk(zz, x, c, k_core, dev(cc=1 - c), src).start()

    def up(zz, src=None):
        @pl.when(z < NZ - 1)
        def _():
            bulk(zz, x, c, 0, dev(zz=lax.min(z + 1, NZ - 1)), src).start()

    def down(zz, src=None):
        @pl.when(z > 0)
        def _():
            bulk(zz, x, c, 1, dev(zz=lax.max(z - 1, 0)), src).start()

    def arrived(zz, xx, cc):
        bulk(zz, xx, cc, 0, dev(cc=1 - c)).wait_recv()

    def hop(s):
        @pl.when(z >= s)
        def _():
            zz = z - s
            arrived(zz, x, c)
            up(zz)
            spread(zz)

        @pl.when(z + s < NZ)
        def _():
            zz = z + s
            arrived(zz, x, c)
            down(zz)
            spread(zz)

    def across(s):
        for p in x_peers:
            for zz, ok in ((z - s, z >= s), (z + s, z + s < NZ)):
                if s == 0:
                    ok = zz >= 0

                @pl.when(ok)
                def _(zz=zz, p=p):
                    arrived(zz, p, c)
                    bulk(zz, p, c, k_core, dev(cc=1 - c)).start()
                if s == 0:
                    break

    def plane_peers():
        out = []
        for kx in range(nx):
            for kz in range(NZ):
                if kx or kz:
                    out.append((lax.rem(z + kz, NZ), lax.rem(x + kx, nx)))
        return out

    chips = plane_peers()
    back = [(lax.rem(z + NZ - kz, NZ), lax.rem(x + nx - kx, nx))
            for kx in range(nx) for kz in range(NZ) if kx or kz]

    def gather_start(buf):
        copies = [push(buf.at[own], buf.at[own], dev(zz=zz, xx=xx)) for zz, xx in chips]
        return copies, [push(buf.at[own], buf.at[own], dev(cc=1 - c))]

    def gather_end(buf, copies, core):
        for copy, (zz, xx) in zip(copies, back):
            copy.wait_recv()
            at = slot(zz, xx, c)
            core.append(push(buf.at[at], buf.at[at], dev(cc=1 - c)))
        for copy in copies:
            copy.wait_send()
        wait(core)

    def all_peers():
        return [lax.rem(m + k, n_mp) for k in range(1, n_mp)]

    def pack(v):
        n = v.shape[0] * rank // 128
        return jnp.concatenate([v[k * n:(k + 1) * n] for k in range(128 // rank)], axis=1)

    def unpack(v):
        return jnp.concatenate([v[:, k * rank:(k + 1) * rank] for k in range(128 // rank)], axis=0)

    qb[own] = q_ref[...].astype(BF16)
    copies, core = gather_start(qb)
    up(z, g_hbm)
    down(z, g_hbm)
    spread(z, g_hbm)
    gather_end(qb, copies, core)

    g_copy.wait()
    gq = jnp.zeros((t, rank), F32)
    for i, s in enumerate(slots):
        gq += dot(g_ref[:, i * f:(i + 1) * f], qb[s], NT)
    gqb[m] = pack(gq)
    copies = [push(gqb.at[m], gqb.at[m], (d, p)) for p in all_peers()]
    e_copy.wait()
    pt = jnp.zeros((rank, f), F32)
    for i, s in enumerate(slots):
        pt += dot(qb[s], e_ref[:, i * f:(i + 1) * f], NT)
    hop(1)
    across(0)
    wait(copies)
    gq_all = jnp.concatenate([unpack(gqb[i]) for i in range(n_mp)], axis=0)
    hi, lo = split(gq_all)
    a = a_ref[...]
    pt += dot(hi, a, TN) + dot(lo, a, TN)
    pb[d] = pt
    wait([push(pb.at[d], pb.at[d], (p, m)) for p in d_peers])
    pt = pb[0]
    for k in range(1, n_dp):
        pt += pb[k]
    pt = pt / n_dp

    p_hi, p_lo = split(pt)
    sums = dot(a, p_hi, NT) + dot(a, p_lo, NT)
    gram = pack(dot(pt, pt, NT, HP))
    nt = t * rank // 128
    for i in range(n_mp):
        sx[i, :nt] = pack(sums[i * t:(i + 1) * t])
        sx[i, nt:] = gram
    rx[m] = sx[m]
    copies = [push(sx.at[p], rx.at[m], (d, p)) for p in all_peers()]
    hop(2)
    across(1)
    wait(copies)
    total = rx[0]
    for i in range(1, n_mp):
        total += rx[i]
    s_own, gram = unpack(total[:nt]), unpack(total[nt:])

    inv = inverse_of_factor(gram)
    pot = dot(inv, pt, NN, HP)
    o_hi, o_lo = split(-pot)
    pp_ref[:rank, :] = o_hi
    pp_ref[rank:, :] = o_lo
    so_hi, so_lo = split(dot(inv, s_own, NT, HP))
    stack = jnp.concatenate([o_hi, o_lo], axis=0)
    s_stack = jnp.concatenate([so_hi, so_lo], axis=0)

    def part(zz, xx, cc):
        cols = pl.ds(pl.multiple_of(((zz * nx + xx) * NC + cc) * f, f), f)
        v = dot(s_stack, g_ref[:, cols], NN) - dot(stack, e_ref[:, cols], NN)
        return v[:rank] + v[rank:]

    copies = []
    for xx in range(nx):
        for zz in range(NZ):
            k = xx * NZ + zz
            s1[k] = part(zz, xx, 1 - c).astype(BF16)
            copies.append(push(s1.at[k], u1.at[k], dev(cc=1 - c)))
    for xx in range(nx):
        for zz in range(NZ):
            qacc[xx * NZ + zz] = part(zz, xx, c)
    wait(copies)
    copies = []
    for k, (zz, xx) in enumerate(chips):
        at = xx * NZ + zz
        s2[k] = (qacc[at] + u1[at].astype(F32)).astype(BF16)
        copies.append(push(s2.at[k], u2.at[k], dev(zz=zz, xx=xx)))
    at = x * NZ + z
    q_sum = qacc[at] + u1[at].astype(F32)
    hop(3)
    across(2)
    wait(copies)
    for k in range(len(chips)):
        q_sum += u2[k].astype(F32)
    qdp[d] = q_sum
    wait([push(qdp.at[d], qdp.at[d], (p, m)) for p in d_peers])
    q_own = qdp[0]
    for k in range(1, n_dp):
        q_own += qdp[k]
    q_own = q_own / n_dp
    qown_ref[...] = q_own

    q2b[own] = q_own.astype(BF16)
    copies, core = gather_start(q2b)
    across(3)
    gather_end(q2b, copies, core)
    for i, s in enumerate(slots):
        qq_ref[:rank, i * f:(i + 1) * f] = q2b[s]
        qq_ref[rank:, i * f:(i + 1) * f] = q2b[s]

    for zz in range(NZ):
        for xx in range(nx):
            arrived(zz, xx, 1 - c)
    for zz in range(NZ):
        @pl.when((zz <= z) & (z < NZ - 1))
        def _(zz=zz):
            bulk(zz, x, c, 0, dev(cc=1 - c)).wait_send()

        @pl.when((zz >= z) & (z > 0))
        def _(zz=zz):
            bulk(zz, x, c, 1, dev(cc=1 - c)).wait_send()
        for k in range(nx - 1):
            bulk(zz, x, c, 2 + k, dev(cc=1 - c)).wait_send()
        for xx in range(nx):
            bulk(zz, xx, c, k_core, dev(cc=1 - c)).wait_send()
    o_copy.wait()


def chain(n_dp, n_mp, attn_out, grad_out, error_buf, q_start):
    t, width = grad_out.shape
    tokens, f = attn_out.shape
    rank = q_start.shape[0]
    nx = n_mp // (NC * NZ)
    half = nx * NZ
    count = 2 * (2 * half - 1) + 2 * (n_mp - 1) + (2 * half - 1) + 2 * (n_dp - 1)
    nt, ng = t * rank // 128, rank * rank // 128
    any_space = pl.BlockSpec(memory_space=pl.ANY)
    vmem = pl.BlockSpec(memory_space=pltpu.VMEM)
    block = (rank, f)
    scratch = [
        pltpu.VMEM((f, width), BF16),
        pltpu.VMEM((t, width), BF16),
        pltpu.VMEM((n_mp,) + block, BF16),
        pltpu.VMEM((n_mp, nt, 128), F32),
        pltpu.VMEM((n_dp,) + block, F32),
        pltpu.VMEM((n_mp, nt + ng, 128), F32),
        pltpu.VMEM((n_mp, nt + ng, 128), F32),
        pltpu.VMEM((half,) + block, F32),
        pltpu.VMEM((n_dp,) + block, F32),
        pltpu.VMEM((n_mp,) + block, BF16),
        pltpu.VMEM((half,) + block, BF16),
        pltpu.VMEM((half,) + block, BF16),
        pltpu.VMEM((half - 1,) + block, BF16),
        pltpu.VMEM((half - 1,) + block, BF16),
        pltpu.SemaphoreType.DMA((count,)),
        pltpu.SemaphoreType.DMA((count,)),
        pltpu.SemaphoreType.DMA((2 + nx, n_mp)),
        pltpu.SemaphoreType.DMA((n_mp,)),
        pltpu.SemaphoreType.DMA((3,)),
    ]
    return pl.pallas_call(
        functools.partial(chain_kernel, n_dp, n_mp, t),
        out_shape=(
            jax.ShapeDtypeStruct((tokens, width), BF16),
            jax.ShapeDtypeStruct((2 * rank, f), BF16),
            jax.ShapeDtypeStruct((2 * rank, width), BF16),
            jax.ShapeDtypeStruct((rank, f), F32),
        ),
        in_specs=[vmem, any_space, any_space, vmem],
        out_specs=(any_space, vmem, vmem, vmem),
        scratch_shapes=scratch,
        compiler_params=pltpu.CompilerParams(
            collective_id=0, has_side_effects=True, vmem_limit_bytes=40 * 2**20),
    )(attn_out, grad_out, error_buf, q_start)


def final_kernel(a_ref, pp_ref, qown_ref, g_ref, w_ref, e_ref, qq_ref,
                 err_ref, q_ref, da_ref, lhs, acc):
    j = pl.program_id(0)
    tokens = a_ref.shape[0]

    @pl.when(j == 0)
    def _():
        lhs[:, :tokens] = jnp.transpose(a_ref[...])
        lhs[:, tokens:] = jnp.transpose(pp_ref[...])
        q_ref[...] = qown_ref[...]
        acc[...] = jnp.zeros_like(acc)

    g = g_ref[...]
    moment = dot(lhs[:, :tokens], g, NN) + e_ref[0].astype(F32)
    err_ref[0] = (moment + dot(lhs[:, tokens:], qq_ref[...], NN)).astype(BF16)
    acc[...] += dot(g, w_ref[...], NT)

    @pl.when(j == pl.num_programs(0) - 1)
    def _():
        da_ref[...] = acc[...].astype(BF16)


def final(attn_out, pp, qown, g_all, proj_weight, error_buf, qq):
    tokens, f = attn_out.shape
    width = g_all.shape[1]
    rank = qown.shape[0]
    n = 1024
    whole = lambda shape: pl.BlockSpec(shape, lambda j: (0,) * len(shape))
    cols = lambda rows: pl.BlockSpec((rows, n), lambda j: (0, j))
    cols3 = pl.BlockSpec((1, f, n), lambda j: (0, 0, j))
    return pl.pallas_call(
        final_kernel,
        grid=(width // n,),
        out_shape=(
            jax.ShapeDtypeStruct((1, f, width), BF16),
            jax.ShapeDtypeStruct((rank, f), F32),
            jax.ShapeDtypeStruct((tokens, f), BF16),
        ),
        in_specs=[whole((tokens, f)), whole((2 * rank, f)), whole((rank, f)),
                  cols(tokens), cols(f), cols3, cols(2 * rank)],
        out_specs=(cols3, whole((rank, f)), whole((tokens, f))),
        scratch_shapes=[pltpu.VMEM((f, tokens + 2 * rank), BF16), pltpu.VMEM((tokens, f), F32)],
        compiler_params=pltpu.CompilerParams(vmem_limit_bytes=40 * 2**20),
    )(attn_out, pp, qown, g_all, proj_weight, error_buf, qq)


def on_device(n_dp, n_mp, attn_out, grad_out, proj_weight, error_buf, q_start):
    g_all, pp, qq, qown = chain(n_dp, n_mp, attn_out, grad_out, error_buf, q_start.T)
    err, q_t, d_attn = final(attn_out, pp, qown, g_all, proj_weight, error_buf, qq)
    return err, q_t.T, d_attn


def solution(mesh):
    in_specs = (
        P("dp", "mp"),
        P(("dp", "mp"), None),
        P("mp", None),
        P("dp", "mp", None),
        P("mp", None),
    )
    out_specs = (P("dp", "mp", None), P("mp", None), P("dp", "mp"))
    return jax.shard_map(
        functools.partial(on_device, mesh.shape["dp"], mesh.shape["mp"]),
        mesh=mesh, in_specs=in_specs, out_specs=out_specs, check_vma=False,
    )
```

```python
import functools

import jax
import jax.numpy as jnp
from jax import lax
from jax.experimental import pallas as pl
from jax.experimental.pallas import tpu as pltpu
from jax.sharding import PartitionSpec as P

MESH = pl.DeviceIdType.MESH
HP = lax.Precision.HIGHEST
F32, BF16 = jnp.float32, jnp.bfloat16
NN = (((1,), (0,)), ((), ()))
NT = (((1,), (1,)), ((), ()))
TN = (((0,), (0,)), ((), ()))
NC, NZ = 2, 4


def dot(a, b, dims, precision=None):
    return lax.dot_general(a, b, dims, precision=precision, preferred_element_type=F32)


def split(v):
    hi = v.astype(BF16)
    return hi, (v - hi.astype(F32)).astype(BF16)


def inverse_of_factor(gram):
    r = gram.shape[0]
    rows = lax.broadcasted_iota(jnp.int32, (r, 1), 0)
    eye = (rows == lax.broadcasted_iota(jnp.int32, (r, r), 1)).astype(F32)
    low, pivots = eye, jnp.ones((r, 1), F32)
    for k in range(r):
        pivot = gram[k:k + 1, k:k + 1]
        pivots = jnp.where(rows == k, pivot, pivots)
        factor = jnp.where(rows > k, gram[:, k:k + 1] / pivot, 0.0)
        low = low - factor * low[k:k + 1, :]
        gram = gram - factor * gram[k:k + 1, :]
    return low * lax.rsqrt(pivots)


def chain_kernel(n_dp, n_mp, t,
                 a_hbm, g_hbm, e_hbm, w_hbm, q_ref,
                 gout, lhs_ref, qq_ref, qown_ref, da_ref,
                 a_ref, e_ref, w_ref, grp, g_ref, qb, gqb, pb, sx, rx, qacc, qdp, q2b, s1, u1, s2, u2,
                 send, recv, gsend, grecv, local):
    nx = n_mp // (NC * NZ)
    half = nx * NZ
    d, m = lax.axis_index("dp"), lax.axis_index("mp")
    c = lax.rem(m, NC)
    x = lax.rem(lax.div(m, NC), nx)
    z = lax.div(m, NC * nx)
    f = a_ref.shape[1]
    rank = q_ref.shape[0]

    def dev(zz=None, xx=None, cc=None):
        zz, xx, cc = (z if zz is None else zz), (x if xx is None else xx), (c if cc is None else cc)
        return (d, (zz * nx + xx) * NC + cc)

    def slot(zz, xx, cc):
        return (cc * nx + xx) * NZ + zz

    slots = [slot(i // (NC * nx), (i // NC) % nx, i % NC) for i in range(n_mp)]
    x_peers = [lax.rem(x + k, nx) for k in range(1, nx)]
    d_peers = [lax.rem(d + k, n_dp) for k in range(1, n_dp)]
    own = slot(z, x, c)

    e_copy = pltpu.make_async_copy(e_hbm.at[0], e_ref, local.at[0])
    g_copy = pltpu.make_async_copy(g_hbm, g_ref, local.at[1])
    own_rows = pl.ds(pl.multiple_of(m * t, t), t)
    o_copy = pltpu.make_async_copy(g_hbm, gout.at[own_rows, :], local.at[2])
    a_copy = pltpu.make_async_copy(a_hbm, a_ref, local.at[3])
    w_copy = pltpu.make_async_copy(w_hbm, w_ref, local.at[4])
    g_copy.start()
    e_copy.start()
    a_copy.start()
    o_copy.start()
    w_copy.start()

    barrier = pltpu.get_barrier_semaphore()
    for k in range(1, n_mp):
        pl.semaphore_signal(barrier, inc=1, device_id=(d, lax.rem(m + k, n_mp)), device_id_type=MESH)
    for p in d_peers:
        pl.semaphore_signal(barrier, inc=1, device_id=(p, m), device_id_type=MESH)
    pl.semaphore_wait(barrier, n_mp - 1 + n_dp - 1)

    used = [0]

    def push(src, dst, peer):
        i = used[0]
        used[0] += 1
        copy = pltpu.make_async_remote_copy(
            src_ref=src, dst_ref=dst, send_sem=send.at[i], recv_sem=recv.at[i],
            device_id=peer, device_id_type=MESH)
        copy.start()
        return copy

    def wait(copies):
        for copy in copies:
            copy.wait()

    def rows_of(zz, xx, cc):
        return pl.ds(pl.multiple_of(((zz * nx + xx) * NC + cc) * t, t), t)

    def bulk(zz, xx, cc, kind, peer, src=None):
        at = gout.at[rows_of(zz, xx, cc), :]
        i = slot(zz, xx, cc)
        return pltpu.make_async_remote_copy(
            src_ref=at if src is None else src, dst_ref=at,
            send_sem=gsend.at[kind, i], recv_sem=grecv.at[i],
            device_id=peer, device_id_type=MESH)

    k_core = 1 + nx

    def spread(zz, src=None):
        for k, p in enumerate(x_peers):
            bulk(zz, x, c, 2 + k, dev(xx=p), src).start()
        bulk(zz, x, c, k_core, dev(cc=1 - c), src).start()

    def up(zz, src=None):
        @pl.when(z < NZ - 1)
        def _():
            bulk(zz, x, c, 0, dev(zz=lax.min(z + 1, NZ - 1)), src).start()

    def down(zz, src=None):
        @pl.when(z > 0)
        def _():
            bulk(zz, x, c, 1, dev(zz=lax.max(z - 1, 0)), src).start()

    def arrived(zz, xx, cc):
        bulk(zz, xx, cc, 0, dev(cc=1 - c)).wait_recv()

    def hop(s):
        @pl.when(z >= s)
        def _():
            zz = z - s
            arrived(zz, x, c)
            up(zz)
            spread(zz)

        @pl.when(z + s < NZ)
        def _():
            zz = z + s
            arrived(zz, x, c)
            down(zz)
            spread(zz)

    def across(s):
        for p in x_peers:
            for zz, ok in ((z - s, z >= s), (z + s, z + s < NZ)):
                if s == 0:
                    ok = zz >= 0

                @pl.when(ok)
                def _(zz=zz, p=p):
                    arrived(zz, p, c)
                    bulk(zz, p, c, k_core, dev(cc=1 - c)).start()
                if s == 0:
                    break

    def plane_peers():
        out = []
        for kx in range(nx):
            for kz in range(NZ):
                if kx or kz:
                    out.append((lax.rem(z + kz, NZ), lax.rem(x + kx, nx)))
        return out

    chips = plane_peers()
    back = [(lax.rem(z + NZ - kz, NZ), lax.rem(x + nx - kx, nx))
            for kx in range(nx) for kz in range(NZ) if kx or kz]

    def gather_start(buf):
        copies = [push(buf.at[own], buf.at[own], dev(zz=zz, xx=xx)) for zz, xx in chips]
        return copies, [push(buf.at[own], buf.at[own], dev(cc=1 - c))]

    def gather_end(buf, copies, core):
        for copy, (zz, xx) in zip(copies, back):
            copy.wait_recv()
            at = slot(zz, xx, c)
            core.append(push(buf.at[at], buf.at[at], dev(cc=1 - c)))
        for copy in copies:
            copy.wait_send()
        wait(core)

    def all_peers():
        return [lax.rem(m + k, n_mp) for k in range(1, n_mp)]

    def pack(v):
        n = v.shape[0] * rank // 128
        return jnp.concatenate([v[k * n:(k + 1) * n] for k in range(128 // rank)], axis=1)

    def unpack(v):
        return jnp.concatenate([v[:, k * rank:(k + 1) * rank] for k in range(128 // rank)], axis=0)

    tz = nx * NC * t

    def group_rows(k):
        return pl.ds(pl.multiple_of(lax.rem(z + k, NZ) * tz, tz), tz)

    def group_load(k):
        zz = lax.rem(z + k, NZ)
        for xx in range(nx):
            arrived(zz, xx, 1 - c)
        copy = pltpu.make_async_copy(gout.at[group_rows(k), :], grp.at[k], local.at[5 + k])
        copy.start()
        return copy

    def group_dot(k, copy):
        copy.wait()
        v = jnp.zeros((tz, f), F32)
        for i in range(0, w_ref.shape[1], 512):
            v += dot(grp[k, :, i:i + 512], w_ref[:, i:i + 512], NT)
        da_ref[group_rows(k), :] = v.astype(BF16)

    qb[own] = q_ref[...].astype(BF16)
    copies, core = gather_start(qb)
    up(z, g_hbm)
    down(z, g_hbm)
    spread(z, g_hbm)
    gather_end(qb, copies, core)

    g_copy.wait()
    gq = jnp.zeros((t, rank), F32)
    for i, s in enumerate(slots):
        gq += dot(g_ref[:, i * f:(i + 1) * f], qb[s], NT)
    gqb[m] = pack(gq)
    copies = [push(gqb.at[m], gqb.at[m], (d, p)) for p in all_peers()]
    e_copy.wait()
    pt = jnp.zeros((rank, f), F32)
    for i, s in enumerate(slots):
        pt += dot(qb[s], e_ref[:, i * f:(i + 1) * f], NT)
    hop(1)
    across(0)
    wait(copies)
    gq_all = jnp.concatenate([unpack(gqb[i]) for i in range(n_mp)], axis=0)
    hi, lo = split(gq_all)
    a_copy.wait()
    a = a_ref[...]
    pt += dot(hi, a, TN) + dot(lo, a, TN)
    pb[d] = pt
    wait([push(pb.at[d], pb.at[d], (p, m)) for p in d_peers])
    pt = pb[0]
    for k in range(1, n_dp):
        pt += pb[k]
    pt = pt / n_dp

    p_hi, p_lo = split(pt)
    sums = dot(a, p_hi, NT) + dot(a, p_lo, NT)
    gram = pack(dot(pt, pt, NT, HP))
    nt = t * rank // 128
    for i in range(n_mp):
        sx[i, :nt] = pack(sums[i * t:(i + 1) * t])
        sx[i, nt:] = gram
    rx[m] = sx[m]
    copies = [push(sx.at[p], rx.at[m], (d, p)) for p in all_peers()]
    o_copy.wait()
    w_copy.wait()
    loaded = group_load(0)
    hop(2)
    across(1)
    group_dot(0, loaded)
    lhs_ref[:, :a_ref.shape[0]] = jnp.transpose(a_ref[...])
    wait(copies)
    total = rx[0]
    for i in range(1, n_mp):
        total += rx[i]
    s_own, gram = unpack(total[:nt]), unpack(total[nt:])

    inv = inverse_of_factor(gram)
    pot = dot(inv, pt, NN, HP)
    o_hi, o_lo = split(-pot)
    so_hi, so_lo = split(dot(inv, s_own, NT, HP))
    stack = jnp.concatenate([o_hi, o_lo], axis=0)
    s_stack = jnp.concatenate([so_hi, so_lo], axis=0)

    def part(zz, xx, cc):
        cols = pl.ds(pl.multiple_of(((zz * nx + xx) * NC + cc) * f, f), f)
        v = dot(s_stack, g_ref[:, cols], NN) - dot(stack, e_ref[:, cols], NN)
        return v[:rank] + v[rank:]

    copies = []
    for xx in range(nx):
        for zz in range(NZ):
            k = xx * NZ + zz
            s1[k] = part(zz, xx, 1 - c).astype(BF16)
            copies.append(push(s1.at[k], u1.at[k], dev(cc=1 - c)))
    for xx in range(nx):
        for zz in range(NZ):
            qacc[xx * NZ + zz] = part(zz, xx, c)
    wait(copies)
    copies = []
    for k, (zz, xx) in enumerate(chips):
        at = xx * NZ + zz
        s2[k] = (qacc[at] + u1[at].astype(F32)).astype(BF16)
        copies.append(push(s2.at[k], u2.at[k], dev(zz=zz, xx=xx)))
    at = x * NZ + z
    q_sum = qacc[at] + u1[at].astype(F32)
    hop(3)
    across(2)
    across(3)
    loaded = [group_load(k) for k in range(1, NZ)]
    group_dot(1, loaded[0])
    wait(copies)
    for k in range(len(chips)):
        q_sum += u2[k].astype(F32)
    qdp[d] = q_sum
    copies = [push(qdp.at[d], qdp.at[d], (p, m)) for p in d_peers]
    group_dot(2, loaded[1])
    wait(copies)
    q_own = qdp[0]
    for k in range(1, n_dp):
        q_own += qdp[k]
    q_own = q_own / n_dp
    qown_ref[...] = q_own

    q2b[own] = q_own.astype(BF16)
    copies, core = gather_start(q2b)
    lhs_ref[:, a_ref.shape[0]:] = jnp.transpose(stack)
    group_dot(3, loaded[2])
    gather_end(q2b, copies, core)
    for i, s in enumerate(slots):
        qq_ref[:rank, i * f:(i + 1) * f] = q2b[s]
        qq_ref[rank:, i * f:(i + 1) * f] = q2b[s]

    for zz in range(NZ):
        @pl.when((zz <= z) & (z < NZ - 1))
        def _(zz=zz):
            bulk(zz, x, c, 0, dev(cc=1 - c)).wait_send()

        @pl.when((zz >= z) & (z > 0))
        def _(zz=zz):
            bulk(zz, x, c, 1, dev(cc=1 - c)).wait_send()
        for k in range(nx - 1):
            bulk(zz, x, c, 2 + k, dev(cc=1 - c)).wait_send()
        for xx in range(nx):
            bulk(zz, xx, c, k_core, dev(cc=1 - c)).wait_send()


def chain(n_dp, n_mp, attn_out, grad_out, error_buf, proj_weight, q_start):
    t, width = grad_out.shape
    tokens, f = attn_out.shape
    rank = q_start.shape[0]
    nx = n_mp // (NC * NZ)
    half = nx * NZ
    count = 2 * (2 * half - 1) + 2 * (n_mp - 1) + (2 * half - 1) + 2 * (n_dp - 1)
    nt, ng = t * rank // 128, rank * rank // 128
    any_space = pl.BlockSpec(memory_space=pl.ANY)
    vmem = pl.BlockSpec(memory_space=pltpu.VMEM)
    block = (rank, f)
    scratch = [
        pltpu.VMEM((tokens, f), BF16),
        pltpu.VMEM((f, width), BF16),
        pltpu.VMEM((f, width), BF16),
        pltpu.VMEM((NZ, tokens // NZ, width), BF16),
        pltpu.VMEM((t, width), BF16),
        pltpu.VMEM((n_mp,) + block, BF16),
        pltpu.VMEM((n_mp, nt, 128), F32),
        pltpu.VMEM((n_dp,) + block, F32),
        pltpu.VMEM((n_mp, nt + ng, 128), F32),
        pltpu.VMEM((n_mp, nt + ng, 128), F32),
        pltpu.VMEM((half,) + block, F32),
        pltpu.VMEM((n_dp,) + block, F32),
        pltpu.VMEM((n_mp,) + block, BF16),
        pltpu.VMEM((half,) + block, BF16),
        pltpu.VMEM((half,) + block, BF16),
        pltpu.VMEM((half - 1,) + block, BF16),
        pltpu.VMEM((half - 1,) + block, BF16),
        pltpu.SemaphoreType.DMA((count,)),
        pltpu.SemaphoreType.DMA((count,)),
        pltpu.SemaphoreType.DMA((2 + nx, n_mp)),
        pltpu.SemaphoreType.DMA((n_mp,)),
        pltpu.SemaphoreType.DMA((5 + NZ,)),
    ]
    return pl.pallas_call(
        functools.partial(chain_kernel, n_dp, n_mp, t),
        out_shape=(
            jax.ShapeDtypeStruct((tokens, width), BF16),
            jax.ShapeDtypeStruct((f, tokens + 2 * rank), BF16),
            jax.ShapeDtypeStruct((2 * rank, width), BF16),
            jax.ShapeDtypeStruct((rank, f), F32),
            jax.ShapeDtypeStruct((tokens, f), BF16),
        ),
        in_specs=[any_space, any_space, any_space, any_space, vmem],
        out_specs=(any_space, vmem, vmem, vmem, vmem),
        scratch_shapes=scratch,
        compiler_params=pltpu.CompilerParams(
            collective_id=0, has_side_effects=True, vmem_limit_bytes=56 * 2**20),
    )(attn_out, grad_out, error_buf, proj_weight, q_start)


def final_kernel(lhs_ref, qown_ref, d_ref, g_ref, e_ref, qq_ref, err_ref, q_ref, da_ref):
    tokens = g_ref.shape[0]

    @pl.when(pl.program_id(0) == 0)
    def _():
        q_ref[...] = qown_ref[...]
        da_ref[...] = d_ref[...]

    moment = dot(lhs_ref[:, :tokens], g_ref[...], NN) + e_ref[0].astype(F32)
    err_ref[0] = (moment + dot(lhs_ref[:, tokens:], qq_ref[...], NN)).astype(BF16)


def final(lhs, qown, d_attn, g_all, error_buf, qq):
    tokens, width = g_all.shape
    rank, f = qown.shape
    n = 1024
    whole = lambda shape: pl.BlockSpec(shape, lambda j: (0,) * len(shape))
    cols = lambda rows: pl.BlockSpec((rows, n), lambda j: (0, j))
    cols3 = pl.BlockSpec((1, f, n), lambda j: (0, 0, j))
    return pl.pallas_call(
        final_kernel,
        grid=(width // n,),
        out_shape=(
            jax.ShapeDtypeStruct((1, f, width), BF16),
            jax.ShapeDtypeStruct((rank, f), F32),
            jax.ShapeDtypeStruct((tokens, f), BF16),
        ),
        in_specs=[whole((f, tokens + 2 * rank)), whole((rank, f)), whole((tokens, f)),
                  cols(tokens), cols3, cols(2 * rank)],
        out_specs=(cols3, whole((rank, f)), whole((tokens, f))),
        compiler_params=pltpu.CompilerParams(vmem_limit_bytes=56 * 2**20),
    )(lhs, qown, d_attn, g_all, error_buf, qq)


def on_device(n_dp, n_mp, attn_out, grad_out, proj_weight, error_buf, q_start):
    g_all, lhs, qq, qown, d_attn = chain(
        n_dp, n_mp, attn_out, grad_out, error_buf, proj_weight, q_start.T)
    err, q_t, d_attn = final(lhs, qown, d_attn, g_all, error_buf, qq)
    return err, q_t.T, d_attn


def solution(mesh):
    in_specs = (
        P("dp", "mp"),
        P(("dp", "mp"), None),
        P("mp", None),
        P("dp", "mp", None),
        P("mp", None),
    )
    out_specs = (P("dp", "mp", None), P("mp", None), P("dp", "mp"))
    return jax.shard_map(
        functools.partial(on_device, mesh.shape["dp"], mesh.shape["mp"]),
        mesh=mesh, in_specs=in_specs, out_specs=out_specs, check_vma=False,
    )
```

```python
import functools

import jax
import jax.numpy as jnp
from jax import lax
from jax.experimental import pallas as pl
from jax.experimental.pallas import tpu as pltpu
from jax.sharding import PartitionSpec as P

MESH = pl.DeviceIdType.MESH
HP = lax.Precision.HIGHEST
F32, BF16 = jnp.float32, jnp.bfloat16
NN = (((1,), (0,)), ((), ()))
NT = (((1,), (1,)), ((), ()))
TN = (((0,), (0,)), ((), ()))
NC, NZ = 2, 4


def dot(a, b, dims, precision=None):
    return lax.dot_general(a, b, dims, precision=precision, preferred_element_type=F32)


def split(v):
    hi = v.astype(BF16)
    return hi, (v - hi.astype(F32)).astype(BF16)


def inverse_of_factor(gram):
    r = gram.shape[0]
    rows = lax.broadcasted_iota(jnp.int32, (r, 1), 0)
    eye = (rows == lax.broadcasted_iota(jnp.int32, (r, r), 1)).astype(F32)
    low, pivots = eye, jnp.ones((r, 1), F32)
    for k in range(r):
        pivot = gram[k:k + 1, k:k + 1]
        pivots = jnp.where(rows == k, pivot, pivots)
        factor = jnp.where(rows > k, gram[:, k:k + 1] / pivot, 0.0)
        low = low - factor * low[k:k + 1, :]
        gram = gram - factor * gram[k:k + 1, :]
    return low * lax.rsqrt(pivots)


def chain_kernel(n_dp, n_mp, t,
                 a_hbm, g_hbm, e_hbm, q_ref,
                 gout, lhs_ref, qown_ref,
                 a_ref, e_ref, qq_ref, g_ref, qb, gqb, pb, sx, rx, qacc, qdp, q2b, s1, u1, s2, u2,
                 send, recv, gsend, grecv, local):
    nx = n_mp // (NC * NZ)
    half = nx * NZ
    d, m = lax.axis_index("dp"), lax.axis_index("mp")
    c = lax.rem(m, NC)
    x = lax.rem(lax.div(m, NC), nx)
    z = lax.div(m, NC * nx)
    f = a_ref.shape[1]
    rank = q_ref.shape[0]

    def dev(zz=None, xx=None, cc=None):
        zz, xx, cc = (z if zz is None else zz), (x if xx is None else xx), (c if cc is None else cc)
        return (d, (zz * nx + xx) * NC + cc)

    def slot(zz, xx, cc):
        return (cc * nx + xx) * NZ + zz

    slots = [slot(i // (NC * nx), (i // NC) % nx, i % NC) for i in range(n_mp)]
    x_peers = [lax.rem(x + k, nx) for k in range(1, nx)]
    d_peers = [lax.rem(d + k, n_dp) for k in range(1, n_dp)]
    own = slot(z, x, c)

    e_copy = pltpu.make_async_copy(e_hbm.at[0], e_ref, local.at[0])
    g_copy = pltpu.make_async_copy(g_hbm, g_ref, local.at[1])
    own_rows = pl.ds(pl.multiple_of(m * t, t), t)
    o_copy = pltpu.make_async_copy(g_hbm, gout.at[own_rows, :], local.at[2])
    a_copy = pltpu.make_async_copy(a_hbm, a_ref, local.at[3])
    g_copy.start()
    e_copy.start()
    a_copy.start()
    o_copy.start()

    barrier = pltpu.get_barrier_semaphore()
    for k in range(1, n_mp):
        pl.semaphore_signal(barrier, inc=1, device_id=(d, lax.rem(m + k, n_mp)), device_id_type=MESH)
    for p in d_peers:
        pl.semaphore_signal(barrier, inc=1, device_id=(p, m), device_id_type=MESH)
    pl.semaphore_wait(barrier, n_mp - 1 + n_dp - 1)

    used = [0]

    def push(src, dst, peer):
        i = used[0]
        used[0] += 1
        copy = pltpu.make_async_remote_copy(
            src_ref=src, dst_ref=dst, send_sem=send.at[i], recv_sem=recv.at[i],
            device_id=peer, device_id_type=MESH)
        copy.start()
        return copy

    def wait(copies):
        for copy in copies:
            copy.wait()

    def rows_of(zz, xx, cc):
        return pl.ds(pl.multiple_of(((zz * nx + xx) * NC + cc) * t, t), t)

    def bulk(zz, xx, cc, kind, peer, src=None):
        at = gout.at[rows_of(zz, xx, cc), :]
        i = slot(zz, xx, cc)
        return pltpu.make_async_remote_copy(
            src_ref=at if src is None else src, dst_ref=at,
            send_sem=gsend.at[kind, i], recv_sem=grecv.at[i],
            device_id=peer, device_id_type=MESH)

    k_core = 1 + nx

    def spread(zz, src=None):
        for k, p in enumerate(x_peers):
            bulk(zz, x, c, 2 + k, dev(xx=p), src).start()
        bulk(zz, x, c, k_core, dev(cc=1 - c), src).start()

    def up(zz, src=None):
        @pl.when(z < NZ - 1)
        def _():
            bulk(zz, x, c, 0, dev(zz=lax.min(z + 1, NZ - 1)), src).start()

    def down(zz, src=None):
        @pl.when(z > 0)
        def _():
            bulk(zz, x, c, 1, dev(zz=lax.max(z - 1, 0)), src).start()

    def arrived(zz, xx, cc):
        bulk(zz, xx, cc, 0, dev(cc=1 - c)).wait_recv()

    def hop(s):
        @pl.when(z >= s)
        def _():
            zz = z - s
            arrived(zz, x, c)
            up(zz)
            spread(zz)

        @pl.when(z + s < NZ)
        def _():
            zz = z + s
            arrived(zz, x, c)
            down(zz)
            spread(zz)

    def across(s):
        for p in x_peers:
            for zz, ok in ((z - s, z >= s), (z + s, z + s < NZ)):
                if s == 0:
                    ok = zz >= 0

                @pl.when(ok)
                def _(zz=zz, p=p):
                    arrived(zz, p, c)
                    bulk(zz, p, c, k_core, dev(cc=1 - c)).start()
                if s == 0:
                    break

    def plane_peers():
        out = []
        for kx in range(nx):
            for kz in range(NZ):
                if kx or kz:
                    out.append((lax.rem(z + kz, NZ), lax.rem(x + kx, nx)))
        return out

    chips = plane_peers()
    back = [(lax.rem(z + NZ - kz, NZ), lax.rem(x + nx - kx, nx))
            for kx in range(nx) for kz in range(NZ) if kx or kz]

    def gather_start(buf):
        copies = [push(buf.at[own], buf.at[own], dev(zz=zz, xx=xx)) for zz, xx in chips]
        return copies, [push(buf.at[own], buf.at[own], dev(cc=1 - c))]

    def gather_end(buf, copies, core):
        for copy, (zz, xx) in zip(copies, back):
            copy.wait_recv()
            at = slot(zz, xx, c)
            core.append(push(buf.at[at], buf.at[at], dev(cc=1 - c)))
        for copy in copies:
            copy.wait_send()
        wait(core)

    def all_peers():
        return [lax.rem(m + k, n_mp) for k in range(1, n_mp)]

    def pack(v):
        n = v.shape[0] * rank // 128
        return jnp.concatenate([v[k * n:(k + 1) * n] for k in range(128 // rank)], axis=1)

    def unpack(v):
        return jnp.concatenate([v[:, k * rank:(k + 1) * rank] for k in range(128 // rank)], axis=0)

    qb[own] = q_ref[...].astype(BF16)
    copies, core = gather_start(qb)
    up(z, g_hbm)
    down(z, g_hbm)
    spread(z, g_hbm)
    gather_end(qb, copies, core)

    g_copy.wait()
    gq = jnp.zeros((t, rank), F32)
    for i, s in enumerate(slots):
        gq += dot(g_ref[:, i * f:(i + 1) * f], qb[s], NT)
    gqb[m] = pack(gq)
    copies = [push(gqb.at[m], gqb.at[m], (d, p)) for p in all_peers()]
    e_copy.wait()
    pt = jnp.zeros((rank, f), F32)
    for i, s in enumerate(slots):
        pt += dot(qb[s], e_ref[:, i * f:(i + 1) * f], NT)
    hop(1)
    across(0)
    wait(copies)
    gq_all = jnp.concatenate([unpack(gqb[i]) for i in range(n_mp)], axis=0)
    hi, lo = split(gq_all)
    a_copy.wait()
    a = a_ref[...]
    pt += dot(hi, a, TN) + dot(lo, a, TN)
    pb[d] = pt
    wait([push(pb.at[d], pb.at[d], (p, m)) for p in d_peers])
    pt = pb[0]
    for k in range(1, n_dp):
        pt += pb[k]
    pt = pt / n_dp

    p_hi, p_lo = split(pt)
    sums = dot(a, p_hi, NT) + dot(a, p_lo, NT)
    gram = pack(dot(pt, pt, NT, HP))
    nt = t * rank // 128
    for i in range(n_mp):
        sx[i, :nt] = pack(sums[i * t:(i + 1) * t])
        sx[i, nt:] = gram
    rx[m] = sx[m]
    copies = [push(sx.at[p], rx.at[m], (d, p)) for p in all_peers()]
    hop(2)
    across(1)
    lhs_ref[:, :a_ref.shape[0]] = jnp.transpose(a_ref[...])
    wait(copies)
    total = rx[0]
    for i in range(1, n_mp):
        total += rx[i]
    s_own, gram = unpack(total[:nt]), unpack(total[nt:])

    inv = inverse_of_factor(gram)
    pot = dot(inv, pt, NN, HP)
    o_hi, o_lo = split(-pot)
    so_hi, so_lo = split(dot(inv, s_own, NT, HP))
    stack = jnp.concatenate([o_hi, o_lo], axis=0)
    s_stack = jnp.concatenate([so_hi, so_lo], axis=0)

    def part(zz, xx, cc):
        cols = pl.ds(pl.multiple_of(((zz * nx + xx) * NC + cc) * f, f), f)
        v = dot(s_stack, g_ref[:, cols], NN) - dot(stack, e_ref[:, cols], NN)
        return v[:rank] + v[rank:]

    copies = []
    for xx in range(nx):
        for zz in range(NZ):
            k = xx * NZ + zz
            s1[k] = part(zz, xx, 1 - c).astype(BF16)
            copies.append(push(s1.at[k], u1.at[k], dev(cc=1 - c)))
    for xx in range(nx):
        for zz in range(NZ):
            qacc[xx * NZ + zz] = part(zz, xx, c)
    wait(copies)
    copies = []
    for k, (zz, xx) in enumerate(chips):
        at = xx * NZ + zz
        s2[k] = (qacc[at] + u1[at].astype(F32)).astype(BF16)
        copies.append(push(s2.at[k], u2.at[k], dev(zz=zz, xx=xx)))
    at = x * NZ + z
    q_sum = qacc[at] + u1[at].astype(F32)
    hop(3)
    across(2)
    across(3)
    wait(copies)
    for k in range(len(chips)):
        q_sum += u2[k].astype(F32)
    qdp[d] = q_sum
    copies = [push(qdp.at[d], qdp.at[d], (p, m)) for p in d_peers]
    wait(copies)
    q_own = qdp[0]
    for k in range(1, n_dp):
        q_own += qdp[k]
    q_own = q_own / n_dp
    qown_ref[...] = q_own

    q2b[own] = q_own.astype(BF16)
    copies, core = gather_start(q2b)
    lhs_ref[:, a_ref.shape[0]:] = jnp.transpose(stack)
    gather_end(q2b, copies, core)
    for i, s in enumerate(slots):
        qq_ref[:rank, i * f:(i + 1) * f] = q2b[s]
        qq_ref[rank:, i * f:(i + 1) * f] = q2b[s]

    q_rows = pltpu.make_async_copy(
        qq_ref, gout.at[pl.ds(a_ref.shape[0], 2 * rank), :], local.at[4])
    q_rows.start()

    for zz in range(NZ):
        for xx in range(nx):
            arrived(zz, xx, 1 - c)
    for zz in range(NZ):
        @pl.when((zz <= z) & (z < NZ - 1))
        def _(zz=zz):
            bulk(zz, x, c, 0, dev(cc=1 - c)).wait_send()

        @pl.when((zz >= z) & (z > 0))
        def _(zz=zz):
            bulk(zz, x, c, 1, dev(cc=1 - c)).wait_send()
        for k in range(nx - 1):
            bulk(zz, x, c, 2 + k, dev(cc=1 - c)).wait_send()
        for xx in range(nx):
            bulk(zz, xx, c, k_core, dev(cc=1 - c)).wait_send()
    o_copy.wait()
    q_rows.wait()


def chain(n_dp, n_mp, attn_out, grad_out, error_buf, q_start):
    t, width = grad_out.shape
    tokens, f = attn_out.shape
    rank = q_start.shape[0]
    nx = n_mp // (NC * NZ)
    half = nx * NZ
    count = 2 * (2 * half - 1) + 2 * (n_mp - 1) + (2 * half - 1) + 2 * (n_dp - 1)
    nt, ng = t * rank // 128, rank * rank // 128
    any_space = pl.BlockSpec(memory_space=pl.ANY)
    vmem = pl.BlockSpec(memory_space=pltpu.VMEM)
    block = (rank, f)
    scratch = [
        pltpu.VMEM((tokens, f), BF16),
        pltpu.VMEM((f, width), BF16),
        pltpu.VMEM((2 * rank, width), BF16),
        pltpu.VMEM((t, width), BF16),
        pltpu.VMEM((n_mp,) + block, BF16),
        pltpu.VMEM((n_mp, nt, 128), F32),
        pltpu.VMEM((n_dp,) + block, F32),
        pltpu.VMEM((n_mp, nt + ng, 128), F32),
        pltpu.VMEM((n_mp, nt + ng, 128), F32),
        pltpu.VMEM((half,) + block, F32),
        pltpu.VMEM((n_dp,) + block, F32),
        pltpu.VMEM((n_mp,) + block, BF16),
        pltpu.VMEM((half,) + block, BF16),
        pltpu.VMEM((half,) + block, BF16),
        pltpu.VMEM((half - 1,) + block, BF16),
        pltpu.VMEM((half - 1,) + block, BF16),
        pltpu.SemaphoreType.DMA((count,)),
        pltpu.SemaphoreType.DMA((count,)),
        pltpu.SemaphoreType.DMA((2 + nx, n_mp)),
        pltpu.SemaphoreType.DMA((n_mp,)),
        pltpu.SemaphoreType.DMA((5,)),
    ]
    return pl.pallas_call(
        functools.partial(chain_kernel, n_dp, n_mp, t),
        out_shape=(
            jax.ShapeDtypeStruct((tokens + 2 * rank, width), BF16),
            jax.ShapeDtypeStruct((f, tokens + 2 * rank), BF16),
            jax.ShapeDtypeStruct((rank, f), F32),
        ),
        in_specs=[any_space, any_space, any_space, vmem],
        out_specs=(any_space, vmem, vmem),
        scratch_shapes=scratch,
        compiler_params=pltpu.CompilerParams(
            collective_id=0, has_side_effects=True, vmem_limit_bytes=56 * 2**20),
    )(attn_out, grad_out, error_buf, q_start)


def final_kernel(lhs_ref, qown_ref, g_ref, w_ref, e_ref, err_ref, q_ref, da_ref, acc):
    j = pl.program_id(0)
    tokens = acc.shape[0]

    @pl.when(j == 0)
    def _():
        q_ref[...] = qown_ref[...]
        acc[...] = jnp.zeros_like(acc)

    err_ref[0] = (dot(lhs_ref[...], g_ref[...], NN) + e_ref[0].astype(F32)).astype(BF16)
    acc[...] += dot(g_ref[:tokens, :], w_ref[...], NT)

    @pl.when(j == pl.num_programs(0) - 1)
    def _():
        da_ref[...] = acc[...].astype(BF16)


def final(tokens, lhs, qown, g_all, proj_weight, error_buf):
    depth, width = g_all.shape
    rank, f = qown.shape
    n = 1024
    whole = lambda shape: pl.BlockSpec(shape, lambda j: (0,) * len(shape))
    cols = lambda rows: pl.BlockSpec((rows, n), lambda j: (0, j))
    cols3 = pl.BlockSpec((1, f, n), lambda j: (0, 0, j))
    return pl.pallas_call(
        final_kernel,
        grid=(width // n,),
        out_shape=(
            jax.ShapeDtypeStruct((1, f, width), BF16),
            jax.ShapeDtypeStruct((rank, f), F32),
            jax.ShapeDtypeStruct((tokens, f), BF16),
        ),
        in_specs=[whole((f, depth)), whole((rank, f)), cols(depth), cols(f), cols3],
        out_specs=(cols3, whole((rank, f)), whole((tokens, f))),
        scratch_shapes=[pltpu.VMEM((tokens, f), F32)],
        compiler_params=pltpu.CompilerParams(vmem_limit_bytes=56 * 2**20),
    )(lhs, qown, g_all, proj_weight, error_buf)


def on_device(n_dp, n_mp, attn_out, grad_out, proj_weight, error_buf, q_start):
    g_all, lhs, qown = chain(n_dp, n_mp, attn_out, grad_out, error_buf, q_start.T)
    err, q_t, d_attn = final(attn_out.shape[0], lhs, qown, g_all, proj_weight, error_buf)
    return err, q_t.T, d_attn


def solution(mesh):
    in_specs = (
        P("dp", "mp"),
        P(("dp", "mp"), None),
        P("mp", None),
        P("dp", "mp", None),
        P("mp", None),
    )
    out_specs = (P("dp", "mp", None), P("mp", None), P("dp", "mp"))
    return jax.shard_map(
        functools.partial(on_device, mesh.shape["dp"], mesh.shape["mp"]),
        mesh=mesh, in_specs=in_specs, out_specs=out_specs, check_vma=False,
    )
```
